32 devices in a mesh: pipe: 4 (over y, core), expert: 8 (over z, x).
Axes of the slice: x: 2, y: 2, z: 4, core: 2. Of those that a mesh axis runs over, the one named last changes fastest.
Arguments:
- fwd_tokens: bfloat16 [4, 64, 3584], P('pipe', 'expert'), may hold values from -6 to 6
- saved_tokens: bfloat16 [2, 4, 64, 3584], P(None, 'pipe', 'expert'), may hold values from -6 to 6
- cotangent: bfloat16 [4, 64, 3584], P('pipe', 'expert'), may hold values from -6 to 6
- fwd_routes: int32 [2, 4, 64, 2], P(None, 'pipe', 'expert'), may hold values from 0 to 3, all different within a row; in each aligned block of 8 rows (0 to 7, 8 to 15, ..., all dimensions but the last counted through in order) at most 5 rows name the same one
- bwd_routes: int32 [2, 4, 64, 2], P(None, 'pipe', 'expert'), may hold values from 0 to 3, all different within a row; in each aligned block of 8 rows (0 to 7, 8 to 15, ..., all dimensions but the last counted through in order) at most 5 rows name the same one
- norm_gain: float32 [4, 3584], P('pipe'), may hold values from 0.1 to 1.9
- router: bfloat16 [4, 3584, 4], P('pipe'), may hold values from -0.09375 to 0.09375
- w_gate: bfloat16 [4, 3584, 4096], P('pipe', None, 'expert'), may hold values from -0.09375 to 0.09375
- w_up: bfloat16 [4, 3584, 4096], P('pipe', None, 'expert'), may hold values from -0.09375 to 0.09375
- w_down: bfloat16 [4, 4096, 3584], P('pipe', 'expert'), may hold values from -0.1875 to 0.1875
Outputs:
- fwd_out: bfloat16 [4, 64, 3584], P('pipe', 'expert')
- bwd_out: bfloat16 [4, 64, 3584], P('pipe', 'expert')
The draws below stay inside these ranges and needn't reach their ends.
Inputs may be any that keep to these rules, and one draw needn't show every extreme that they name: `fwd_routes`: each row names 2 different experts. In every aligned block of 8 rows (one device's tokens of one step and section) no expert is named more than 5 times; in at least one block some expert is named exactly 5 times. `bwd_routes`: each row names 2 different experts. In every aligned block of 8 rows (one device's tokens of one step and section) no expert is named more than 5 times; in at least one block some expert is named exactly 5 times.
All inputs are finite; a program needn't handle non-finite values.
Results may differ from the reference program's by a relative error of at most 0.018.
Values may be sent and summed in bfloat16 or wider, within the bound.
A program may use at most 64 MiB of HBM per device.

```python
import math
import jax
import jax.numpy as jnp
import numpy as np
from jax import lax

D = 3584
FFE = 1024
TOP = 2
EXPERTS = 4
TICKS = 2
TOK_DEV = 8
CAP = 5
TOKENS = 64
SECTIONS = 4
N_EXPERT = 8


def level_of(key, extent, shards, smallest, top_value):
    def one(dim, shards_of):
        steps = jax.random.uniform(jax.random.fold_in(jax.random.fold_in(key, 6), dim), (shards_of,), jnp.float32, smallest / len(shards), top_value / len(shards))
        return jnp.repeat(jnp.exp(steps), extent[dim] // shards_of).reshape((-1,) + (1,) * (len(extent) - dim - 1))

    factor_of = one(*shards[0])
    for cut in shards[1:]:
        factor_of = factor_of * one(*cut)
    return factor_of


def shared_out(own_key, own, number, rows, number_of, top, bound, slope):
    sequence = jax.random.permutation(own_key, number_of)
    crowded, usual = portions_of(number_of, rows * top, bound, slope, True), portions_of(number_of, rows * top, bound, slope, False)
    places = jnp.arange(number_of)

    def named(lengths, offset_by):
        used = int((lengths > 0).sum())
        fixed = max(1, used // 4)
        shifted = fixed + (places - fixed + offset_by * (used - fixed)) % max(1, number_of - fixed)
        return jnp.zeros((number_of,), jnp.int32).at[sequence[jnp.where(places < fixed, places, shifted)]].set(jnp.asarray(lengths, jnp.int32))

    lengths = jnp.where(number % 4 == 0, named(crowded, number // 4), named(usual, number - number // 4 - 1))
    mixed = jax.random.permutation(jax.random.fold_in(own, 3), number_of)
    source_of, taker = mixed[0:number_of // 2 * 2:2], mixed[1:number_of // 2 * 2:2]
    slack = jnp.minimum(lengths[source_of] - 1, bound - lengths[taker]) // 2
    slack = jnp.where((source_of == sequence[0]) | (taker == sequence[0]) | (lengths[taker] == 0), 0, jnp.maximum(slack, 0))
    shifted = jax.random.randint(jax.random.fold_in(own, 4), (number_of // 2,), 0, 1 << 20) % (slack + 1)
    lengths = lengths.at[source_of].add(-shifted).at[taker].add(shifted)
    items = jnp.searchsorted(jnp.cumsum(lengths), jnp.arange(rows * top), side="right").astype(jnp.int32)
    listing = items.reshape(top, rows).T
    listing = listing[jax.random.permutation(jax.random.fold_in(own, 1), rows)]
    offset_by = jax.random.randint(jax.random.fold_in(own, 2), (rows, 1), 0, top)
    return jnp.take_along_axis(listing, (jnp.arange(top)[None, :] + offset_by) % top, axis=1)


def portions_of(count, total, most, slope, full):
    weights = [(1 << 20) // math.isqrt(standing ** slope) + 1 for standing in range(1, count + 1)]
    largest = most if full else min(most, max(-(-total // count), total * weights[0] // sum(weights)))
    least = 1 if total - largest >= count - 1 else 0
    holding, surplus = [largest] + [least] * (count - 1), total - largest - least * (count - 1)
    while surplus > 0:
        free = [i for i in range(1, count) if holding[i] < largest] or [i for i in range(1, count) if holding[i] < most]
        whole, remaining = sum([weights[i] for i in free]), surplus
        for i in free:
            more = min(most - holding[i], max(1, remaining * weights[i] // whole), surplus)
            holding[i] = holding[i] + more
            surplus = surplus - more
    return np.array(holding)


def normal_values(rng, shape, width, reach, pieces=(), kind=jnp.bfloat16):
    level = level_of(rng, shape, pieces, -0.22, 0.18) if pieces else 1.0
    values = jax.random.normal(rng, shape, jnp.float32) * width * level
    return jnp.minimum(jnp.maximum(values, -reach), reach).astype(kind)


def setup_inputs(seed: int = 0) -> dict:
    streams_of = jax.random.split(jax.random.key(seed), 11)
    fwd_tokens = normal_values(streams_of[0], (SECTIONS, TOKENS, D), 1.0, 6.0, ((0, 4), (1, 8)))
    saved_tokens = normal_values(streams_of[1], (TICKS, SECTIONS, TOKENS, D), 1.0, 6.0, ((1, 4), (2, 8)))
    cotangent = normal_values(streams_of[2], (SECTIONS, TOKENS, D), 1.0, 6.0, ((0, 4), (1, 8)))
    fwd_routes_keys = jax.random.split(jax.random.fold_in(streams_of[3], 1), TICKS * SECTIONS * TOKENS // TOK_DEV)
    fwd_routes_turns = jax.random.permutation(jax.random.fold_in(streams_of[3], 3), TICKS * SECTIONS * TOKENS // TOK_DEV)
    fwd_routes = jax.vmap(lambda own, number: shared_out(jax.random.fold_in(streams_of[3], 2), own, number, TOK_DEV, EXPERTS, TOP, CAP, 1))(fwd_routes_keys, fwd_routes_turns).reshape((TICKS, SECTIONS, TOKENS, TOP))
    bwd_routes_keys = jax.random.split(jax.random.fold_in(streams_of[4], 1), TICKS * SECTIONS * TOKENS // TOK_DEV)
    bwd_routes_turns = jax.random.permutation(jax.random.fold_in(streams_of[4], 3), TICKS * SECTIONS * TOKENS // TOK_DEV)
    bwd_routes = jax.vmap(lambda own, number: shared_out(jax.random.fold_in(streams_of[4], 2), own, number, TOK_DEV, EXPERTS, TOP, CAP, 1))(bwd_routes_keys, bwd_routes_turns).reshape((TICKS, SECTIONS, TOKENS, TOP))
    norm_gain = jnp.clip(1.0 + 0.18 * jax.random.normal(streams_of[5], (SECTIONS, D), jnp.float32), 0.1, 1.9)
    router = normal_values(streams_of[6], (SECTIONS, D, EXPERTS), D ** -0.5, 0.09375, ((0, 4),))
    w_gate = normal_values(streams_of[7], (SECTIONS, D, EXPERTS * FFE), D ** -0.5, 0.09375, ((0, 4), (2, 8)))
    w_up = normal_values(streams_of[8], (SECTIONS, D, EXPERTS * FFE), D ** -0.5, 0.09375, ((0, 4), (2, 8)))
    w_down = normal_values(streams_of[9], (SECTIONS, EXPERTS * FFE, D), FFE ** -0.5, 0.1875, ((0, 4), (1, 8)))
    return {"fwd_tokens": fwd_tokens, "saved_tokens": saved_tokens, "cotangent": cotangent, "fwd_routes": fwd_routes, "bwd_routes": bwd_routes, "norm_gain": norm_gain, "router": router, "w_gate": w_gate, "w_up": w_up, "w_down": w_down}


def norm_rows(values, norm_gain):
    wide = values.astype(jnp.float32)
    scale = lax.rsqrt(lax.optimization_barrier(jnp.mean(wide * wide, axis=-1, keepdims=True)) + 1e-06)
    return wide * scale * norm_gain.astype(jnp.float32)

def gate_values(normed, router_w, routes, expert_count):
    logits = jnp.dot(normed, router_w, preferred_element_type=jnp.float32)
    sig_all = jax.nn.sigmoid(logits)
    route_pick = (routes[..., None] == jnp.arange(expert_count, dtype=jnp.int32)).astype(jnp.float32)
    chosen = lax.optimization_barrier(jnp.sum(route_pick * sig_all[:, None, :], axis=-1))
    gate_total = lax.optimization_barrier(jnp.sum(chosen, axis=-1, keepdims=True))
    gate_share = chosen / gate_total
    return (chosen, gate_total, gate_share, route_pick)

def slot_matrix(routes, expert_count, cap_rows):
    flat_routes = routes.reshape(-1).astype(jnp.int32)
    hit_table = (flat_routes[:, None] == jnp.arange(expert_count, dtype=jnp.int32)).astype(jnp.int32)
    before = jnp.cumsum(hit_table, axis=0) - hit_table
    slot_index = lax.optimization_barrier(jnp.sum(before * hit_table, axis=1))
    position = flat_routes * cap_rows + slot_index
    placement = (position[:, None] == jnp.arange(expert_count * cap_rows, dtype=jnp.int32)).astype(jnp.float32)
    return placement.reshape(routes.shape[0], routes.shape[1], expert_count * cap_rows)

def expert_forward(row_block, gate_w, up_w, down_w):
    gate_pre = jnp.dot(row_block, gate_w, preferred_element_type=jnp.float32)
    up_pre = jnp.dot(row_block, up_w, preferred_element_type=jnp.float32)
    hidden = (jax.nn.silu(gate_pre) * up_pre).astype(jnp.bfloat16)
    return jnp.dot(hidden, down_w, preferred_element_type=jnp.float32).astype(jnp.bfloat16)

def expert_backward(row_block, cotan_rows, gate_w, up_w, down_w):
    gate_pre = jnp.dot(row_block, gate_w, preferred_element_type=jnp.float32)
    up_pre = jnp.dot(row_block, up_w, preferred_element_type=jnp.float32)
    gate_sig = jax.nn.sigmoid(gate_pre)
    gate_act = gate_pre * gate_sig
    hidden = (gate_act * up_pre).astype(jnp.bfloat16)
    expert_out = jnp.dot(hidden, down_w, preferred_element_type=jnp.float32).astype(jnp.bfloat16)
    hidden_grad = jnp.einsum('rd,fd->rf', cotan_rows, down_w, preferred_element_type=jnp.float32)
    gate_grad = (hidden_grad * up_pre * gate_sig * (1.0 + gate_pre * (1.0 - gate_sig))).astype(jnp.bfloat16)
    up_grad = (hidden_grad * gate_act).astype(jnp.bfloat16)
    row_grad = jnp.einsum('rf,df->rd', gate_grad, gate_w, preferred_element_type=jnp.float32)
    row_grad = row_grad + jnp.einsum('rf,df->rd', up_grad, up_w, preferred_element_type=jnp.float32)
    return (row_grad.astype(jnp.bfloat16), expert_out)

def token_grad(saved, cotan, norm_gain, router_w, chosen, gate_total, gate_share, route_pick, dgate, row_sum):
    dchosen = (dgate - lax.optimization_barrier(jnp.sum(gate_share * dgate, axis=-1, keepdims=True))) / gate_total
    logit_grad = dchosen * chosen * (1.0 - chosen)
    logit_full = jnp.einsum('tk,tke->te', logit_grad, route_pick, precision=lax.Precision.HIGHEST)
    router_back = jnp.dot(logit_full, router_w.astype(jnp.float32).T, precision=lax.Precision.HIGHEST)
    _, norm_pull = jax.vjp(lambda values: norm_rows(values, norm_gain), saved.astype(jnp.float32))
    return (cotan.astype(jnp.float32) + norm_pull(row_sum + router_back)[0]).astype(jnp.bfloat16)

def to_experts(buffer):
    return buffer.reshape(N_EXPERT, EXPERTS, CAP, D).transpose(1, 0, 2, 3).reshape(EXPERTS, N_EXPERT * CAP, D)

def part_weights(gate_w, up_w, down_w):
    split_count = N_EXPERT // EXPERTS
    part_units = FFE // split_count
    gate_parts = gate_w.reshape(D, EXPERTS, split_count, part_units).transpose(1, 2, 0, 3)
    up_parts = up_w.reshape(D, EXPERTS, split_count, part_units).transpose(1, 2, 0, 3)
    down_parts = down_w.reshape(EXPERTS, split_count, part_units, D)
    return (gate_parts, up_parts, down_parts)

def unfold_parts(partial_value):
    split_count = N_EXPERT // EXPERTS
    return partial_value.reshape(EXPERTS, split_count, N_EXPERT, CAP, D).astype(jnp.float32)

def section_step(packed):
    tokens_in, saved, cotan, routes_f, routes_b, norm_gain, router_w, gate_w, up_w, down_w = packed
    gate_parts, up_parts, down_parts = part_weights(gate_w, up_w, down_w)
    normed = norm_rows(tokens_in, norm_gain).astype(jnp.bfloat16)
    chosen_f, total_f, share_f, pick_f = gate_values(normed, router_w, routes_f, EXPERTS)
    gb_f = share_f.astype(jnp.bfloat16).astype(jnp.float32)
    place_f = jax.vmap(lambda block: slot_matrix(block, EXPERTS, CAP))(routes_f.reshape(N_EXPERT, TOK_DEV, TOP))
    spread_f = lax.optimization_barrier(jnp.sum(place_f, axis=2))
    weighted_f = lax.optimization_barrier(jnp.sum(place_f * gb_f.reshape(N_EXPERT, TOK_DEV, TOP, 1), axis=2))
    send_f = jnp.einsum('ntp,ntd->npd', spread_f, normed.astype(jnp.float32).reshape(N_EXPERT, TOK_DEV, D)).astype(jnp.bfloat16)

    def forward_expert(item):
        expert_rows, gate_e, up_e, down_e = item
        return lax.map(lambda part: expert_forward(expert_rows, part[0], part[1], part[2]), (gate_e, up_e, down_e))
    out_f = unfold_parts(lax.map(forward_expert, (to_experts(send_f), gate_parts, up_parts, down_parts)))
    weighted_four = weighted_f.reshape(N_EXPERT, TOK_DEV, EXPERTS, CAP)
    mixture = jnp.einsum('ntec,ejncd->ntd', weighted_four, out_f, precision=lax.Precision.HIGHEST).reshape(TOKENS, D)
    fwd_result = (tokens_in.astype(jnp.float32) + mixture).astype(jnp.bfloat16)
    saved_norm = norm_rows(saved, norm_gain).astype(jnp.bfloat16)
    chosen_b, total_b, share_b, pick_b = gate_values(saved_norm, router_w, routes_b, EXPERTS)
    gb_b = share_b.astype(jnp.bfloat16).astype(jnp.float32)
    place_b = jax.vmap(lambda block: slot_matrix(block, EXPERTS, CAP))(routes_b.reshape(N_EXPERT, TOK_DEV, TOP))
    spread_b = lax.optimization_barrier(jnp.sum(place_b, axis=2))
    weighted_b = lax.optimization_barrier(jnp.sum(place_b * gb_b.reshape(N_EXPERT, TOK_DEV, TOP, 1), axis=2))
    cot_blocks = cotan.astype(jnp.float32).reshape(N_EXPERT, TOK_DEV, D)
    send_m = jnp.einsum('ntp,ntd->npd', spread_b, saved_norm.astype(jnp.float32).reshape(N_EXPERT, TOK_DEV, D)).astype(jnp.bfloat16)
    send_c = jnp.einsum('ntp,ntd->npd', weighted_b, cot_blocks).astype(jnp.bfloat16)

    def backward_expert(item):
        expert_rows, expert_cot, gate_e, up_e, down_e = item
        return lax.map(lambda part: expert_backward(expert_rows, expert_cot, part[0], part[1], part[2]), (gate_e, up_e, down_e))
    grad_e, out_e = lax.map(backward_expert, (to_experts(send_m), to_experts(send_c), gate_parts, up_parts, down_parts))
    grad_back = unfold_parts(grad_e)
    out_back = unfold_parts(out_e)
    spread_four = spread_b.reshape(N_EXPERT, TOK_DEV, EXPERTS, CAP)
    row_sum = jnp.einsum('ntec,ejncd->ntd', spread_four, grad_back, precision=lax.Precision.HIGHEST).reshape(TOKENS, D)
    place_five = place_b.reshape(N_EXPERT, TOK_DEV, TOP, EXPERTS, CAP)
    out_route = jnp.einsum('ntkec,ejncd->ntkd', place_five, out_back, precision=lax.Precision.HIGHEST).reshape(TOKENS, TOP, D)
    dgate = lax.optimization_barrier(jnp.sum(out_route * cotan.astype(jnp.float32)[:, None, :], axis=-1))
    bwd_result = token_grad(saved, cotan, norm_gain, router_w, chosen_b, total_b, share_b, pick_b, dgate, row_sum)
    return (fwd_result, bwd_result)

def reference(fwd_tokens, saved_tokens, cotangent, fwd_routes, bwd_routes, norm_gain, router, w_gate, w_up, w_down):
    forward_in = fwd_tokens
    cotan_in = cotangent
    for tick_index in range(TICKS):
        fwd_result, bwd_result = lax.map(section_step, (forward_in, saved_tokens[tick_index], cotan_in, fwd_routes[tick_index], bwd_routes[tick_index], norm_gain, router, w_gate, w_up, w_down))
        if tick_index + 1 < TICKS:
            forward_in = jnp.roll(fwd_result, 1, axis=0)
            cotan_in = jnp.roll(bwd_result, -1, axis=0)
    return (fwd_result, bwd_result)
```

```python
import jax
import jax.numpy as jnp
from jax import lax
from jax.sharding import PartitionSpec as P

F32 = jnp.float32
BF16 = jnp.bfloat16


def from_behind(block, axis, distance):
    devices = range(lax.axis_size(axis))
    route = [((i - distance) % len(devices), i) for i in devices]
    return lax.ppermute(block, axis, route)


def norm_rows(values, norm_gain):
    wide = values.astype(F32)
    scale = lax.rsqrt(jnp.mean(wide * wide, axis=-1, keepdims=True) + 1e-06)
    return wide * scale * norm_gain


def slots_of(hit):
    count = hit.shape[1]
    earlier = jnp.arange(count)[:, None] > jnp.arange(count)[None, :]
    return jnp.sum(jnp.where(earlier[None, :, :], hit[:, None, :], 0.0), axis=2)


def expert_place(hit, cap_rows):
    slot = slots_of(hit)
    lines = jnp.arange(cap_rows, dtype=F32)[None, :, None]
    return jnp.where((slot[:, None, :] == lines) & (hit[:, None, :] > 0), 1.0, 0.0)


def local(
    fwd_tokens,
    saved_tokens,
    cotangent,
    fwd_routes,
    bwd_routes,
    norm_gain,
    router,
    w_gate,
    w_up,
    w_down,
):
    x_in = fwd_tokens[0]
    c_in = cotangent[0]
    gain = norm_gain[0]
    router_w = router[0]
    gate_w, up_w, down_w = w_gate[0], w_up[0], w_down[0]
    ticks = saved_tokens.shape[0]
    tok, width = x_in.shape
    top = fwd_routes.shape[-1]
    experts = router_w.shape[1]
    cap = 5 * tok * top // (4 * experts)
    blocks = lax.axis_size("expert")
    split = blocks // experts
    mine = (lax.axis_index("expert") // split).astype(F32)
    rows = blocks * cap

    def gather(block):
        return lax.all_gather(block, "expert", axis=0, tiled=False)

    route_cols = jnp.concatenate(
        [fwd_routes[:, 0], bwd_routes[:, 0]], axis=0
    )
    route_cols = route_cols.transpose(1, 0, 2).reshape(tok, 2 * ticks * top).astype(BF16)
    route_cols = jnp.pad(route_cols, ((0, 0), (0, 128 - 2 * ticks * top)))
    wide_x = jnp.concatenate([x_in, route_cols], axis=1)
    zeros = jnp.zeros((2 * tok, 128), BF16)
    rest = jnp.concatenate([jnp.concatenate([saved_tokens[0, 0], c_in], axis=0), zeros], axis=1)
    first = gather(jnp.concatenate([wide_x, rest], axis=0))
    routes_all = (
        first[:, :tok, width : width + 2 * ticks * top]
        .astype(F32)
        .reshape(blocks, tok, 2 * ticks, top)
    )
    later = [None] + [gather(saved_tokens[t, 0]) for t in range(1, ticks)]

    def packed(values, routes):
        normed = norm_rows(values, gain).astype(BF16)
        logits = jnp.dot(
            normed.reshape(blocks * tok, width), router_w, preferred_element_type=F32
        ).reshape(blocks, tok, experts)
        sig = jax.nn.sigmoid(logits)
        pick = jnp.sum(
            (routes[..., None] == jnp.arange(experts, dtype=F32)).astype(F32), axis=2
        )
        total = jnp.sum(pick * sig, axis=-1)
        own = (jnp.arange(experts, dtype=F32) == mine).astype(F32)
        hit = jnp.sum(pick * own, axis=-1)
        share = jnp.sum(pick * sig * own, axis=-1) / total
        share = share.astype(BF16).astype(F32)
        place = expert_place(hit, cap)
        gate_rows = jnp.sum(place * share[:, None, :], axis=-1).reshape(rows, 1)
        place = place.astype(BF16)
        taken = jnp.einsum("npt,ntd->npd", place, normed, preferred_element_type=F32)
        return taken.astype(BF16).reshape(rows, width), gate_rows, place

    def owner_place(routes):
        pick = (routes[..., None] == jnp.arange(experts, dtype=jnp.int32)).astype(F32)
        hit = jnp.sum(pick, axis=1)
        slot = slots_of(hit.T)
        line = (slot.T[:, :, None] == jnp.arange(cap, dtype=F32)).astype(F32)
        spot = pick[:, :, :, None, None] * line[:, None, :, None, :]
        spot = jnp.broadcast_to(spot, (tok, top, experts, split, cap))
        return spot.reshape(tok, top, rows), pick

    for t in range(ticks):
        saved = saved_tokens[t, 0]
        if t == 0:
            x_all = first[:, :tok, :width]
            z_all = first[:, tok : 2 * tok, :width]
            c_all = first[:, 2 * tok :, :width]
        else:
            both = gather(jnp.concatenate([x_in, c_in], axis=0))
            x_all, c_all = both[:, :tok], both[:, tok:]
            z_all = later[t]
        m_rows, gate_b, place_b = packed(z_all, routes_all[:, :, ticks + t])
        c_rows = jnp.einsum("npt,ntd->npd", place_b, c_all, preferred_element_type=F32)
        c_rows = c_rows.astype(BF16).reshape(rows, width)
        u_rows, gate_f, _ = packed(x_all, routes_all[:, :, t])
        stacked = jnp.concatenate([u_rows, m_rows], axis=0)
        a = jnp.dot(stacked, gate_w, preferred_element_type=F32)
        b = jnp.dot(stacked, up_w, preferred_element_type=F32)
        sig_a = jax.nn.sigmoid(a)
        act = a * sig_a
        hidden = (act * b).astype(BF16)
        out = jnp.dot(hidden[:rows], down_w, preferred_element_type=F32) * gate_f
        raw_grad = jnp.einsum("rd,fd->rf", c_rows, down_w, preferred_element_type=F32)
        dgate_rows = jnp.sum(raw_grad * hidden[rows:].astype(F32), axis=1, keepdims=True)
        hidden_grad = raw_grad * gate_b
        a_b, b_b, sig_b, act_b = a[rows:], b[rows:], sig_a[rows:], act[rows:]
        gate_grad = (hidden_grad * b_b * sig_b * (1.0 + a_b * (1.0 - sig_b))).astype(BF16)
        up_grad = (hidden_grad * act_b).astype(BF16)
        row_grad = jnp.einsum("rf,df->rd", gate_grad, gate_w, preferred_element_type=F32)
        row_grad = row_grad + jnp.einsum("rf,df->rd", up_grad, up_w, preferred_element_type=F32)
        high = dgate_rows.astype(BF16)
        low = (dgate_rows - high.astype(F32)).astype(BF16)
        tail = jnp.pad(jnp.concatenate([high, low], axis=1), ((0, 0), (0, 126)))
        reply = jnp.concatenate([out.astype(BF16), row_grad.astype(BF16), tail], axis=1)
        span = reply.shape[1]
        reply = reply.reshape(blocks, cap * span // 128, 128)
        back = lax.all_to_all(reply, "expert", split_axis=0, concat_axis=0, tiled=True)
        back = back.reshape(rows, span)

        spot_f, _ = owner_place(fwd_routes[t, 0])
        spot_b, pick_b = owner_place(bwd_routes[t, 0])
        mixture = jnp.dot(
            jnp.sum(spot_f, axis=1).astype(BF16), back[:, :width], preferred_element_type=F32
        )
        row_sum = jnp.dot(
            jnp.sum(spot_b, axis=1).astype(BF16),
            back[:, width : 2 * width],
            preferred_element_type=F32,
        )
        dgate_got = jnp.sum(back[:, 2 * width : 2 * width + 2].astype(F32), axis=1)
        dgate = jnp.sum(spot_b * dgate_got, axis=-1)
        y = (x_in.astype(F32) + mixture).astype(BF16)

        normed_b = norm_rows(saved, gain).astype(BF16)
        sig_own = jax.nn.sigmoid(jnp.dot(normed_b, router_w, preferred_element_type=F32))
        chosen = jnp.sum(pick_b * sig_own[:, None, :], axis=-1)
        total = jnp.sum(chosen, axis=-1, keepdims=True)
        share = chosen / total
        dchosen = (dgate - jnp.sum(share * dgate, axis=-1, keepdims=True)) / total
        logit_grad = dchosen * chosen * (1.0 - chosen)
        logit_full = jnp.sum(logit_grad[..., None] * pick_b, axis=1)
        router_back = jnp.dot(
            logit_full, router_w.astype(F32).T, precision=lax.Precision.HIGHEST
        )
        _, norm_pull = jax.vjp(lambda values: norm_rows(values, gain), saved.astype(F32))
        dz = (c_in.astype(F32) + norm_pull(row_sum + router_back)[0]).astype(BF16)
        if t + 1 < ticks:
            x_in = from_behind(y, "pipe", 1)
            c_in = from_behind(dz, "pipe", -1)
    return (y[None], dz[None])


def solution(mesh):
    return jax.shard_map(
        local,
        mesh=mesh,
        in_specs=(
            P("pipe", "expert", None),
            P(None, "pipe", "expert", None),
            P("pipe", "expert", None),
            P(None, "pipe", "expert", None),
            P(None, "pipe", "expert", None),
            P("pipe", None),
            P("pipe", None, None),
            P("pipe", None, "expert"),
            P("pipe", None, "expert"),
            P("pipe", "expert", None),
        ),
        out_specs=(P("pipe", "expert", None), P("pipe", "expert", None)),
        check_vma=False,
    )
```
